32 devices in a mesh: seq: 8 (over z, y), head: 4 (over x, core).
Axes of the slice: x: 2, y: 2, z: 4, core: 2. Of those that a mesh axis runs over, the one named last changes fastest.
Arguments:
- residual: bfloat16 [1024, 8192], P('seq', 'head'), may hold values from -45 to 45
- key_gate: bfloat16 [1024, 8192], P('seq', 'head'), may hold values from -6 to 6
- query_gate: bfloat16 [1024, 8192], P('seq', 'head'), may hold values from -6 to 6
- norm_gain: float32 [8192], P('head'), may hold values from 0.1 to 1.9
- filters: float32 [8192, 128], P('head'), may hold values from -0.5 to 0.5
- hyena_cotangent: bfloat16 [1024, 8192], P('seq', 'head'), may hold values from -6 to 6
- attn_query: bfloat16 [1024, 4096], P('seq', 'head'), may hold values from -6 to 6
- attention_keys: bfloat16 [1024, 512], P('seq', 'head'), may hold values from -6 to 6
- attention_values: bfloat16 [1024, 512], P('seq', 'head'), may hold values from -6 to 6
- attn_cotangent: bfloat16 [1024, 4096], P('seq', 'head'), may hold values from -6 to 6
- doc_ids: int32 [1024], P('seq'), may hold values from 0 to 3, never falling along the last dimension, each value on 1 to 768 neighbouring positions
Outputs:
- grad_residual: bfloat16 [1024, 8192], P('seq', 'head')
- grad_key_gate: bfloat16 [1024, 8192], P('seq', 'head')
- grad_query_gate: bfloat16 [1024, 8192], P('seq', 'head')
- grad_gain: float32 [8192], P('head')
- grad_filters: float32 [8192, 128], P('head')
- grad_query: bfloat16 [1024, 4096], P('seq', 'head')
- key_gradient: bfloat16 [1024, 512], P('seq', 'head')
- value_gradient: bfloat16 [1024, 512], P('seq', 'head')
The draws below stay inside these ranges and needn't reach their ends.
Inputs may be any that keep to these rules, and one draw needn't show every extreme that they name: `doc_ids`: document ids never fall along the sequence; each document holds 1 to 768 tokens, and one holds exactly 768.
All inputs are finite; a program needn't handle non-finite values.
Results may differ from the reference program's by a relative error of at most 0.0076.
Values may be sent and summed in bfloat16 or wider, within the bound.
A program may use at most 64 MiB of HBM per device.

```python
import math
import jax
import jax.numpy as jnp
import numpy as np
from jax import lax

D = 8192
QUERY_HEADS = 32
KEY_VALUE_HEADS = 4
HEAD_SIZE = 128
FLEN = 128
DOCS = 4
TOKEN_COUNT = 1024
DOC_MOST = 768


def draw_residual(key, part):
    key = jax.random.fold_in(key, 5)
    random_subkeys = jax.random.split(key, 3)
    col_frac = jnp.arange(D, dtype=jnp.float32)[None, :] / D
    wobble = jnp.exp(jax.random.uniform(random_subkeys[1], (1, D), jnp.float32, -0.35, 0.35))
    row_scale = jnp.exp(jax.random.uniform(random_subkeys[2], (TOKEN_COUNT, 1), jnp.float32, 0.0, math.log(10.0)))
    base_random_key = jnp.clip(jax.random.normal(random_subkeys[0], (TOKEN_COUNT, D), jnp.float32), -6.0, 6.0)
    col_scale = 0.05 * jnp.power(10.0, col_frac) * wobble
    return (base_random_key * row_scale * col_scale).astype(jnp.bfloat16)


def draw_attention_keys(key, part):
    key = jax.random.fold_in(key, 7)
    base_random_key = jnp.clip(jax.random.normal(key, (TOKEN_COUNT, KEY_VALUE_HEADS * HEAD_SIZE), jnp.float32), -6.0, 6.0)
    return base_random_key.astype(jnp.bfloat16)


def draw_attn_query(key, part):
    key = jax.random.fold_in(key, 9)
    base_random_key = jnp.clip(jax.random.normal(key, (TOKEN_COUNT, QUERY_HEADS * HEAD_SIZE), jnp.float32), -6.0, 6.0)
    return base_random_key.astype(jnp.bfloat16)


def level_of(rng, extent, cuts, least, largest):
    def one(axis_at, shards_of):
        heights = jax.random.uniform(jax.random.fold_in(jax.random.fold_in(rng, 6), axis_at), (shards_of,), jnp.float32, least / len(cuts), largest / len(cuts))
        return jnp.repeat(jnp.exp(heights), extent[axis_at] // shards_of).reshape((-1,) + (1,) * (len(extent) - axis_at - 1))

    factor_of = one(*cuts[0])
    for cut in cuts[1:]:
        factor_of = factor_of * one(*cut)
    return factor_of


def profile(number_of, total, reach, lean):
    weights = [(1 << 20) // math.isqrt(rank ** lean) + 1 for rank in range(2, number_of + 1)]
    surplus, counts = total - reach - (number_of - 1), [1] * (number_of - 1)
    while surplus > 0:
        movable = [i for i in range(number_of - 1) if counts[i] < reach]
        whole, remaining = sum([weights[i] for i in movable]), surplus
        for i in movable:
            more = min(reach - counts[i], max(1, remaining * weights[i] // whole), surplus)
            counts[i] = counts[i] + more
            surplus = surplus - more
    return np.array([reach] + counts)


def uneven_parts(rng, count, total, bound, slope):
    if count == 2:
        one = jax.random.randint(rng, (), max(1, total - bound), min(bound, total - 1) + 1)
        return jnp.stack([one, total - one])
    sizes = jnp.asarray(profile(count, total, bound, slope), jnp.int32)
    pairs = (count - 1) // 2
    giver, receiver = sizes[1:1 + 2 * pairs:2], sizes[2:2 + 2 * pairs:2]
    margin = jnp.minimum(giver - 1, bound - receiver)
    moved = jax.random.randint(jax.random.fold_in(rng, 1), (pairs,), 0, 1 << 20) % (margin + 1)
    sizes = sizes.at[1:1 + 2 * pairs:2].set(giver - moved).at[2:2 + 2 * pairs:2].set(receiver + moved)
    return sizes[jax.random.permutation(jax.random.fold_in(rng, 2), count)]


def gaussian(key, shape, deviation, reach, shards=(), kind=jnp.bfloat16):
    array = jax.random.normal(key, shape, jnp.float32) * deviation
    if len(shards) > 0:
        array = level_of(key, shape, shards, -0.22, 0.18) * array
    return jnp.clip(array, min=-reach, max=reach).astype(kind)


def setup_inputs(seed: int = 0) -> dict:
    keys = jax.random.split(jax.random.key(seed), 12)
    return {
        "residual": draw_residual(jax.random.fold_in(keys[11], 71), 0),
        "key_gate": gaussian(keys[1], (TOKEN_COUNT, D), 1.0, 6.0, ((0, 8), (1, 4))),
        "query_gate": gaussian(keys[2], (TOKEN_COUNT, D), 1.0, 6.0, ((0, 8), (1, 4))),
        "norm_gain": jnp.clip(1.0 + 0.18 * jax.random.normal(keys[3], (D,), jnp.float32), 0.1, 1.9),
        "filters": gaussian(keys[4], (D, FLEN), FLEN ** -0.5, 0.5, ((0, 4),), jnp.float32),
        "hyena_cotangent": gaussian(keys[5], (TOKEN_COUNT, D), 1.0, 6.0, ((0, 8), (1, 4))),
        "attn_query": draw_attn_query(jax.random.fold_in(keys[11], 71), 0),
        "attention_keys": draw_attention_keys(jax.random.fold_in(keys[11], 71), 0),
        "attention_values": gaussian(keys[8], (TOKEN_COUNT, KEY_VALUE_HEADS * HEAD_SIZE), 1.0, 6.0, ((0, 8), (1, 4))),
        "attn_cotangent": gaussian(keys[9], (TOKEN_COUNT, QUERY_HEADS * HEAD_SIZE), 1.0, 6.0, ((0, 8), (1, 4))),
        "doc_ids": jnp.searchsorted(jnp.cumsum(uneven_parts(keys[10], DOCS, TOKEN_COUNT, DOC_MOST, 2)), jnp.arange(TOKEN_COUNT), side="right").astype(jnp.int32),
    }


NORM_EPS = 1e-05

def forward_filter(signal, filters):
    length = signal.shape[0]
    padded = jnp.pad(signal, ((FLEN - 1, 0), (0, 0)))
    taps_t = filters.T

    def one_tap(tap_number, total):
        window = lax.dynamic_slice_in_dim(padded, (FLEN - 1 - tap_number).astype(jnp.int32), length, 0)
        weights = lax.dynamic_index_in_dim(taps_t, tap_number, 0, keepdims=True)
        return total + window * weights
    return lax.fori_loop(0, FLEN, one_tap, jnp.zeros_like(signal))

def backward_filter(signal, filters):
    length = signal.shape[0]
    padded = jnp.pad(signal, ((0, FLEN - 1), (0, 0)))
    taps_t = filters.T

    def one_tap(tap_number, total):
        window = lax.dynamic_slice_in_dim(padded, tap_number.astype(jnp.int32), length, 0)
        weights = lax.dynamic_index_in_dim(taps_t, tap_number, 0, keepdims=True)
        return total + window * weights
    return lax.fori_loop(0, FLEN, one_tap, jnp.zeros_like(signal))

def filter_grad(gated_in, upstream):
    length = gated_in.shape[0]
    padded = jnp.pad(gated_in, ((FLEN - 1, 0), (0, 0)))

    def one_tap(tap_number, table):
        window = lax.dynamic_slice_in_dim(padded, (FLEN - 1 - tap_number).astype(jnp.int32), length, 0)
        row_sum = lax.optimization_barrier(jnp.sum(upstream * window, axis=0))[None, :]
        return lax.dynamic_update_slice_in_dim(table, row_sum, tap_number.astype(jnp.int32), 0)
    table = lax.fori_loop(0, FLEN, one_tap, jnp.zeros((FLEN, gated_in.shape[1]), gated_in.dtype))
    return table.T

def hyena_grads(residual, key_gate, query_gate, norm_gain, filters, hyena_cotangent):
    signal_rows = residual.astype(jnp.float32)
    inverse = lax.rsqrt(lax.optimization_barrier(jnp.mean(signal_rows * signal_rows, axis=1, keepdims=True)) + NORM_EPS)
    normed = signal_rows * inverse
    scaled = normed * norm_gain
    gates_k = key_gate.astype(jnp.float32)
    gated_rows = (scaled * gates_k).astype(jnp.bfloat16)
    gated_f = lax.optimization_barrier(gated_rows).astype(jnp.float32)
    filtered = forward_filter(gated_f, filters)
    upstream = hyena_cotangent.astype(jnp.float32)
    grad_query_gate = (upstream * filtered).astype(jnp.bfloat16)
    inner_grad = (upstream * query_gate.astype(jnp.float32)).astype(jnp.bfloat16)
    inner_f = lax.optimization_barrier(inner_grad).astype(jnp.float32)
    back_conv = backward_filter(inner_f, filters)
    grad_key_gate = (back_conv * scaled).astype(jnp.bfloat16)
    grad_scaled = back_conv * gates_k
    grad_gain = lax.optimization_barrier(jnp.sum(grad_scaled * normed, axis=0))
    along_rows = lax.optimization_barrier(jnp.sum(norm_gain * grad_scaled * normed, axis=1, keepdims=True))
    grad_residual = (inverse * (norm_gain * grad_scaled - normed * along_rows / D)).astype(jnp.bfloat16)
    grad_filters = filter_grad(gated_f, inner_f)
    return (grad_residual, grad_key_gate, grad_query_gate, grad_gain, grad_filters)

def attention_grads(attn_query, attention_keys, attention_values, attn_cotangent, doc_ids):
    token_total = attn_query.shape[0]
    query_group_width = QUERY_HEADS // KEY_VALUE_HEADS
    score_scale = HEAD_SIZE ** (-0.5)
    position = jnp.arange(token_total, dtype=jnp.int32)
    allowed = (position[:, None] >= position[None, :]) & (doc_ids[:, None] == doc_ids[None, :])
    q_heads = attn_query.reshape(token_total, QUERY_HEADS, HEAD_SIZE).transpose(1, 0, 2)
    d_heads = attn_cotangent.reshape(token_total, QUERY_HEADS, HEAD_SIZE).transpose(1, 0, 2)
    key_heads = attention_keys.reshape(token_total, KEY_VALUE_HEADS, HEAD_SIZE).transpose(1, 0, 2)
    value_heads = attention_values.reshape(token_total, KEY_VALUE_HEADS, HEAD_SIZE).transpose(1, 0, 2)

    def one_head(inputs):
        query_head, cot_head, head_number = inputs
        key_head = lax.dynamic_index_in_dim(key_heads, head_number // query_group_width, 0, keepdims=False)
        value_head = lax.dynamic_index_in_dim(value_heads, head_number // query_group_width, 0, keepdims=False)
        scores = jnp.dot(query_head, key_head.T, preferred_element_type=jnp.float32) * score_scale
        scores = jnp.where(allowed, scores, -jnp.inf)
        probs = jax.nn.softmax(scores, axis=1)
        dprobs = jnp.dot(cot_head, value_head.T, preferred_element_type=jnp.float32)
        row_delta = lax.optimization_barrier(jnp.sum(probs * dprobs, axis=1, keepdims=True))
        value_gradient = jnp.dot(probs.astype(jnp.bfloat16).T, cot_head, preferred_element_type=jnp.float32)
        dscores = (probs * (dprobs - row_delta)).astype(jnp.bfloat16)
        grad_query = jnp.dot(dscores, key_head, preferred_element_type=jnp.float32) * score_scale
        key_gradient = jnp.dot(dscores.T, query_head, preferred_element_type=jnp.float32) * score_scale
        return (grad_query, key_gradient, value_gradient)
    grads_q, key_gradients, value_gradients = lax.map(one_head, (q_heads, d_heads, jnp.arange(QUERY_HEADS, dtype=jnp.int32)))
    grad_query = grads_q.transpose(1, 0, 2).reshape(token_total, QUERY_HEADS * HEAD_SIZE).astype(jnp.bfloat16)
    key_gradient = key_gradients.reshape(KEY_VALUE_HEADS, query_group_width, token_total, HEAD_SIZE).sum(axis=1).transpose(1, 0, 2).reshape(token_total, KEY_VALUE_HEADS * HEAD_SIZE).astype(jnp.bfloat16)
    value_gradient = value_gradients.reshape(KEY_VALUE_HEADS, query_group_width, token_total, HEAD_SIZE).sum(axis=1).transpose(1, 0, 2).reshape(token_total, KEY_VALUE_HEADS * HEAD_SIZE).astype(jnp.bfloat16)
    return (grad_query, key_gradient, value_gradient)

def reference(residual, key_gate, query_gate, norm_gain, filters, hyena_cotangent, attn_query, attention_keys, attention_values, attn_cotangent, doc_ids):
    grad_residual, grad_key_gate, grad_query_gate, grad_gain, grad_filters = hyena_grads(residual, key_gate, query_gate, norm_gain, filters, hyena_cotangent)
    grad_query, key_gradient, value_gradient = attention_grads(attn_query, attention_keys, attention_values, attn_cotangent, doc_ids)
    return (grad_residual, grad_key_gate, grad_query_gate, grad_gain, grad_filters, grad_query, key_gradient, value_gradient)
```

```python
import functools

import jax
import jax.numpy as jnp
import ml_dtypes
import numpy as np
from jax import lax
from jax.experimental import pallas as pl
from jax.experimental.pallas import tpu as pltpu
from jax.sharding import PartitionSpec as P

HEAD = 128
NORM_EPS = 1e-05
FLOOR = -1e30
CHUNK = 512
F32 = jnp.float32
BF16 = jnp.bfloat16
MESH = pl.DeviceIdType.MESH


def split_const(x):
    high = x.astype(ml_dtypes.bfloat16)
    low = (x - high.astype(np.float64)).astype(ml_dtypes.bfloat16)
    return high, low


def dft_tables(rows):
    size = 2 * rows
    freq = 2 * np.pi * (np.arange(rows) + 0.5) / size
    angle = freq[:, None] * np.arange(size)[None, :]
    forward = np.concatenate([np.cos(angle), -np.sin(angle)], 0)
    back = np.concatenate([np.cos(angle[:, :rows]), -np.sin(angle[:, :rows])], 0).T * (2.0 / size)
    near = split_const(forward[:, :rows])
    far = split_const(forward[:, rows:])
    inverse = split_const(back)
    return near + far + inverse


def split(x):
    high = x.astype(BF16)
    return high, (x - high.astype(F32)).astype(BF16)


def dot(a, b):
    return lax.dot_general(a, b, (((1,), (0,)), ((), ())), preferred_element_type=F32)


def dot_t(a, b):
    return lax.dot_general(a, b, (((1,), (1,)), ((), ())), preferred_element_type=F32)


def wide(x, times):
    return jnp.concatenate([x] * times, axis=1)


def kernel(
    n, nh, model, cg, rg, rh, w,
    res, kgate, qgate, gain, filt, cot, query, keys, values, dout, docs,
    dnh, dnl, dfh, dfl, eh, el,
    g_res, g_kg, g_qg, g_gain, g_filt, g_q, g_k, g_v,
    inner_s, inner_h, gated_s, gated_h, f_s, g_s, gs_s,
    kvd, qt, dt, qf, df, dq, sbuf, rbuf, rs_src, rs_dst, ag, sq, al,
    in_ss, in_rs, ga_ss, ga_rs, kv_ss, kv_rs, dk_ss, dk_rs, rs_ss, rs_rs, ag_ss, ag_rs,
    sq_ss, sq_rs, al_ss, al_rs,
):
    me = lax.axis_index("seq")
    hd = lax.axis_index("head")
    rows, channels = res.shape
    chunks = channels // CHUNK
    heads = query.shape[1] // HEAD
    scale = HEAD ** (-0.5)

    def cols(c):
        return pl.ds(pl.multiple_of(c * CHUNK, CHUNK), CHUNK)

    def remote(src, dst, ss, rs, seq, head):
        return pltpu.make_async_remote_copy(
            src_ref=src, dst_ref=dst, send_sem=ss, recv_sem=rs,
            device_id=(seq, head), device_id_type=MESH,
        )

    def each(count, body):
        def step(j, _):
            body(j)
            return 0
        lax.fori_loop(0, count, step, 0)

    def others(count, mine, body):
        def step(j):
            @pl.when(j != mine)
            def _():
                body(j)
        each(count, step)

    barrier = pltpu.get_barrier_semaphore()
    others(n, me, lambda j: pl.semaphore_signal(barrier, inc=1, device_id=(j, hd), device_id_type=MESH))
    others(nh, hd, lambda j: pl.semaphore_signal(barrier, inc=1, device_id=(me, j), device_id_type=MESH))

    kvd[me, 0:rows, :] = keys[...]
    kvd[me, rows : 2 * rows, :] = values[...]
    kvd[me, 2 * rows : 2 * rows + 16, :] = jnp.broadcast_to(docs[...].astype(F32), (16, rows)).astype(BF16)

    def square_step(i, acc):
        x = res[:, pl.ds(pl.multiple_of(i * 128, 128), 128)].astype(F32)
        return acc + x * x

    part = lax.fori_loop(0, channels // 128, square_step, jnp.zeros((rows, 128), F32))
    sq[hd] = jnp.broadcast_to(jnp.sum(part.T, axis=0, keepdims=True), (8, rows))

    pl.semaphore_wait(barrier, n - 1 + nh - 1)

    def sq_copy(slot, peer):
        return remote(sq.at[slot], sq.at[slot], sq_ss.at[peer], sq_rs.at[slot], me, peer)

    def al_copy(slot, peer):
        return remote(al.at[slot], al.at[slot], al_ss.at[peer], al_rs.at[slot], me, peer)

    def kv_copy(slot, peer):
        return remote(kvd.at[slot], kvd.at[slot], kv_ss.at[peer], kv_rs.at[slot], peer, hd)

    others(nh, hd, lambda j: sq_copy(hd, j).start())

    def send_kv(j):
        @pl.when(j > me)
        def _():
            kv_copy(me, j).start()
    each(n, send_kv)

    prev = jnp.maximum(me - 1, 0)
    succ = jnp.minimum(me + 1, n - 1)

    def in_copy(c):
        return remote(inner_s.at[c], inner_h.at[c], in_ss.at[c], in_rs.at[c], prev, hd)

    def ga_copy(c):
        return remote(gated_s.at[c], gated_h.at[c], ga_ss.at[c], ga_rs.at[c], succ, hd)

    def make_inner(c):
        inner_s[c] = (cot[:, cols(c)].astype(F32) * qgate[:, cols(c)].astype(F32)).astype(BF16)

        @pl.when(me > 0)
        def _():
            in_copy(c).start()
    each(chunks, make_inner)

    @pl.when(me == n - 1)
    def _():
        inner_h[...] = jnp.zeros_like(inner_h)

    @pl.when(me == 0)
    def _():
        gated_h[...] = jnp.zeros_like(gated_h)

    def filter_spectrum(c):
        block = filt[pl.ds(pl.multiple_of(c * CHUNK, CHUNK), CHUNK), :]
        fh, fl = split(block)
        f_s[c] = dot_t(dnh[...], fh) + (dot_t(dnh[...], fl) + dot_t(dnl[...], fh))
    each(chunks, filter_spectrum)

    others(nh, hd, lambda j: sq_copy(j, j).wait_recv())
    total = sq[0]
    for j in range(1, nh):
        total = total + sq[j]
    inv_row = lax.rsqrt(total * (1.0 / model) + NORM_EPS)
    inv = jnp.broadcast_to(inv_row[0:1, :], (128, rows)).T

    def norm_of(c):
        return res[:, cols(c)].astype(F32) * wide(inv, CHUNK // 128)

    def make_gated(c):
        scaled = norm_of(c) * gain[:, cols(c)]
        gated = (scaled * kgate[:, cols(c)].astype(F32)).astype(BF16)
        gated_s[c] = gated

        @pl.when(me < n - 1)
        def _():
            ga_copy(c).start()
        g_s[c] = dot(dnh[...], gated) + dot(dnl[...], gated)
    each(chunks, make_gated)

    for h in range(heads):
        span = slice(h * HEAD, (h + 1) * HEAD)
        span_rows = slice(h * rows, (h + 1) * rows)
        q = query[:, span]
        d = dout[:, span]
        qf[span_rows, :] = q
        df[span_rows, :] = d
        qt[:, span_rows] = q.astype(F32).T.astype(BF16)
        dt[:, span_rows] = d.astype(F32).T.astype(BF16)

    my_docs = jnp.broadcast_to(docs[...].astype(F32), (rows, rows))
    row_at = lax.broadcasted_iota(jnp.int32, (rows, rows), 0)
    col_at = lax.broadcasted_iota(jnp.int32, (rows, rows), 1)

    def scores_of(j):
        key_docs = jnp.broadcast_to(kvd[j, 2 * rows : 2 * rows + 16, :].astype(F32)[0:1, :], (rows, rows)).T
        allowed = (key_docs == my_docs) & ((row_at <= col_at) | (j < me))
        bias = jnp.where(allowed, 0.0, FLOOR)
        return dot(kvd[j, 0:rows, :], qt[...]) * scale + wide(bias, heads)

    def wait_kv(j):
        @pl.when(j < me)
        def _():
            kv_copy(j, j).wait_recv()

    def max_step(j, top):
        wait_kv(j)
        return jnp.maximum(top, jnp.max(scores_of(j), axis=0, keepdims=True))

    flat = heads * rows
    top = lax.fori_loop(0, me + 1, max_step, jnp.full((1, flat), FLOOR, F32))

    def sum_step(j, state):
        total_p, total_w = state
        p = jnp.exp(scores_of(j) - top)
        dp = dot(kvd[j, rows : 2 * rows, :], dt[...])
        return (
            total_p + jnp.sum(p, axis=0, keepdims=True),
            total_w + jnp.sum(p * dp, axis=0, keepdims=True),
        )

    zero = jnp.zeros((1, flat), F32)
    total_p, total_w = lax.fori_loop(0, me + 1, sum_step, (zero, zero))
    inv_p = 1.0 / total_p
    delta = total_w * inv_p

    dq[...] = jnp.zeros_like(dq)

    def dk_copy(peer, slot):
        return remote(sbuf.at[peer], rbuf.at[slot], dk_ss.at[peer], dk_rs.at[slot], peer, hd)

    def grad_step(j, acc):
        p = jnp.exp(scores_of(j) - top) * inv_p
        dp = dot(kvd[j, rows : 2 * rows, :], dt[...])
        ds = (p * (dp - delta)).astype(BF16)
        dv = dot(p.astype(BF16), df[...])
        dk = dot(ds, qf[...]) * scale
        key_t = kvd[j, 0:rows, :].astype(F32).T.astype(BF16)
        dq[...] += dot(key_t, ds)
        both = jnp.concatenate([dk, dv], axis=0)
        sbuf[j] = both.astype(BF16)

        @pl.when(j < me)
        def _():
            dk_copy(j, me).start()
        return both

    own = lax.fori_loop(0, me + 1, grad_step, jnp.zeros((2 * rows, HEAD), F32))
    for h in range(heads):
        g_q[:, h * HEAD : (h + 1) * HEAD] = (dq[:, h * rows : (h + 1) * rows].T * scale).astype(BF16)

    def synth(re, im):
        sh, sl = split(jnp.concatenate([re, im], axis=0))
        return dot(eh[...], sh) + (dot(eh[...], sl) + dot(el[...], sh))

    def back_step(c, acc):
        @pl.when(me < n - 1)
        def _():
            in_copy(c).wait_recv()
        mine = inner_s[c]
        far = inner_h[c]
        u = (dot(dnh[...], mine) + dot(dfh[...], far)) + (dot(dnl[...], mine) + dot(dfl[...], far))
        ur, ui = u[:rows], u[rows:]
        gr, gi = g_s[c, 0:rows, :], g_s[c, rows : 2 * rows, :]
        taps = synth(ur * gr + ui * gi, ui * gr - ur * gi)
        fr, fi = f_s[c, 0:rows, :], f_s[c, rows : 2 * rows, :]
        back = synth(ur * fr + ui * fi, ui * fr - ur * fi)
        normed = norm_of(c)
        weight = gain[:, cols(c)]
        g_kg[:, cols(c)] = (back * (normed * weight)).astype(BF16)
        gs = back * kgate[:, cols(c)].astype(F32)
        gs_s[c] = gs
        prod = gs * normed
        gain_row = jnp.sum(prod, axis=0, keepdims=True)
        full = jnp.concatenate([taps, jnp.broadcast_to(gain_row, (rg * rh - rows, CHUNK))], axis=0).astype(BF16)
        per = CHUNK // w
        for a in range(per):
            for r in range(rg):
                rs_src[r * cg + c * per + a] = full[r * rh : (r + 1) * rh, a * w : (a + 1) * w]
        prod = prod * weight
        for a in range(CHUNK // 128):
            acc = acc + prod[:, a * 128 : (a + 1) * 128]
        return acc

    along = lax.fori_loop(0, chunks, back_step, jnp.zeros((rows, 128), F32))
    al[hd] = jnp.broadcast_to(jnp.sum(along.T, axis=0, keepdims=True), (8, rows))
    others(nh, hd, lambda j: al_copy(hd, j).start())

    def rs_copy(peer, slot):
        return remote(rs_src.at[peer], rs_dst.at[slot], rs_ss.at[peer], rs_rs.at[slot], peer, hd)

    def ag_copy(slot, peer):
        return remote(ag.at[slot], ag.at[slot], ag_ss.at[peer], ag_rs.at[slot], peer, hd)

    others(n, me, lambda j: rs_copy(j, me).start())

    def query_gate_step(c):
        @pl.when(me > 0)
        def _():
            ga_copy(c).wait_recv()
        far = gated_h[c]
        wv = g_s[c] - (dot(dfh[...], far) + dot(dfl[...], far))
        wr, wi = wv[:rows], wv[rows:]
        fr, fi = f_s[c, 0:rows, :], f_s[c, rows : 2 * rows, :]
        filtered = synth(wr * fr - wi * fi, wr * fi + wi * fr)
        g_qg[:, cols(c)] = (cot[:, cols(c)].astype(F32) * filtered).astype(BF16)
    each(chunks, query_gate_step)

    def rs_step(j, acc):
        rs_copy(j, j).wait_recv()
        return acc + rs_dst[j].astype(F32)

    mine = rs_src[me].astype(F32)
    mine = lax.fori_loop(0, me, rs_step, mine)
    mine = lax.fori_loop(me + 1, n, rs_step, mine)
    ag[me] = mine.astype(BF16)
    others(n, me, lambda j: ag_copy(me, j).start())

    others(nh, hd, lambda j: al_copy(j, j).wait_recv())
    along_sum = al[0]
    for j in range(1, nh):
        along_sum = along_sum + al[j]
    along_col = jnp.broadcast_to(along_sum[0:1, :] * (1.0 / model), (128, rows)).T

    def res_step(c):
        times = CHUNK // 128
        out = gain[:, cols(c)] * gs_s[c] - norm_of(c) * wide(along_col, times)
        g_res[:, cols(c)] = (wide(inv, times) * out).astype(BF16)
    each(chunks, res_step)

    def dk_step(j, acc):
        dk_copy(j, j).wait_recv()
        return acc + rbuf[j].astype(F32)

    own = lax.fori_loop(me + 1, n, dk_step, own)
    g_k[...] = own[:rows].astype(BF16)
    g_v[...] = own[rows:].astype(BF16)

    others(n, me, lambda j: ag_copy(j, j).wait_recv())

    def out_step(g):
        full = jnp.concatenate([ag[r * cg + g].astype(F32) for r in range(rg)], axis=0)
        g_filt[pl.ds(pl.multiple_of(g * w, w), w), :] = full[:rows].T
        g_gain[:, pl.ds(pl.multiple_of(g * w, w), w)] = full[rows : rows + 1]
    each(cg, out_step)

    others(nh, hd, lambda j: sq_copy(hd, j).wait_send())
    others(nh, hd, lambda j: al_copy(hd, j).wait_send())

    def sent_kv(j):
        @pl.when(j > me)
        def _():
            kv_copy(me, j).wait_send()

        @pl.when(j < me)
        def _():
            dk_copy(j, me).wait_send()
    each(n, sent_kv)

    def sent_halo(c):
        @pl.when(me > 0)
        def _():
            in_copy(c).wait_send()

        @pl.when(me < n - 1)
        def _():
            ga_copy(c).wait_send()
    each(chunks, sent_halo)
    others(n, me, lambda j: rs_copy(j, me).wait_send())
    others(n, me, lambda j: ag_copy(me, j).wait_send())


def on_device(n, nh, *args):
    (res, kgate, qgate, gain, filt, cot, query, keys, values, dout, docs) = args
    rows, channels = res.shape
    heads = query.shape[1] // HEAD
    chunks = channels // CHUNK
    cg = min(n, channels // 128)
    rg = n // cg
    w = channels // cg
    rh = -(-(filt.shape[1] + 1) // (16 * rg)) * 16
    size = 2 * rows
    flat = heads * rows
    tables = [jnp.asarray(t) for t in dft_tables(rows)]
    vmem = pl.BlockSpec(memory_space=pltpu.VMEM)
    dma = pltpu.SemaphoreType.DMA
    outs = (
        jax.ShapeDtypeStruct(res.shape, BF16),
        jax.ShapeDtypeStruct(res.shape, BF16),
        jax.ShapeDtypeStruct(res.shape, BF16),
        jax.ShapeDtypeStruct((1, channels), F32),
        jax.ShapeDtypeStruct(filt.shape, F32),
        jax.ShapeDtypeStruct(query.shape, BF16),
        jax.ShapeDtypeStruct(keys.shape, BF16),
        jax.ShapeDtypeStruct(values.shape, BF16),
    )
    block = (chunks, rows, CHUNK)
    scratch = [
        pltpu.VMEM(block, BF16),
        pltpu.VMEM(block, BF16),
        pltpu.VMEM(block, BF16),
        pltpu.VMEM(block, BF16),
        pltpu.VMEM((chunks, size, CHUNK), F32),
        pltpu.VMEM((chunks, size, CHUNK), F32),
        pltpu.VMEM(block, F32),
        pltpu.VMEM((n, size + 16, HEAD), BF16),
        pltpu.VMEM((HEAD, flat), BF16),
        pltpu.VMEM((HEAD, flat), BF16),
        pltpu.VMEM((flat, HEAD), BF16),
        pltpu.VMEM((flat, HEAD), BF16),
        pltpu.VMEM((HEAD, flat), F32),
        pltpu.VMEM((n, size, HEAD), BF16),
        pltpu.VMEM((n, size, HEAD), BF16),
        pltpu.VMEM((n, rh, w), BF16),
        pltpu.VMEM((n, rh, w), BF16),
        pltpu.VMEM((n, rh, w), BF16),
        pltpu.VMEM((nh, 8, rows), F32),
        pltpu.VMEM((nh, 8, rows), F32),
    ]
    scratch += [dma((chunks,))] * 4 + [dma((n,))] * 8 + [dma((nh,))] * 4
    result = pl.pallas_call(
        functools.partial(kernel, n, nh, nh * channels, cg, rg, rh, w),
        out_shape=outs,
        in_specs=[vmem] * (11 + len(tables)),
        out_specs=(vmem,) * len(outs),
        scratch_shapes=scratch,
        compiler_params=pltpu.CompilerParams(
            collective_id=0, has_side_effects=True, vmem_limit_bytes=56 * 1024 * 1024
        ),
        name="hyena_attention_backward",
    )(
        res, kgate, qgate, gain.reshape(1, channels), filt, cot, query, keys, values, dout,
        docs.reshape(1, rows), *tables,
    )
    return result[:3] + (result[3].reshape(channels),) + result[4:]


def solution(mesh):
    n, nh = mesh.shape["seq"], mesh.shape["head"]
    rows = P("seq", "head")
    return jax.shard_map(
        functools.partial(on_device, n, nh),
        mesh=mesh,
        in_specs=(rows, rows, rows, P("head"), P("head", None), rows, rows, rows, rows, rows, P("seq")),
        out_specs=(rows, rows, rows, P("head"), P("head", None), rows, rows, rows),
        check_vma=False,
    )
```

```python
import functools

import jax
import jax.numpy as jnp
import ml_dtypes
import numpy as np
from jax import lax
from jax.experimental import pallas as pl
from jax.experimental.pallas import tpu as pltpu
from jax.sharding import PartitionSpec as P

HEAD = 128
NORM_EPS = 1e-05
FLOOR = -1e30
CHUNK = 512
F32 = jnp.float32
BF16 = jnp.bfloat16
MESH = pl.DeviceIdType.MESH


def split_const(x):
    high = x.astype(ml_dtypes.bfloat16)
    low = (x - high.astype(np.float64)).astype(ml_dtypes.bfloat16)
    return high, low


def dft_tables(rows):
    size = 2 * rows
    freq = 2 * np.pi * (np.arange(rows) + 0.5) / size
    angle = freq[:, None] * np.arange(size)[None, :]
    forward = np.concatenate([np.cos(angle), -np.sin(angle)], 0)
    wave = angle[:, :rows].T
    back = np.concatenate([np.cos(wave), -np.sin(wave)], 0) * (2.0 / size)
    near = split_const(forward[:, :rows])
    far = split_const(forward[:, rows:])
    inverse = split_const(back)
    return near + far + inverse


def split(x):
    high = x.astype(BF16)
    return high, (x - high.astype(F32)).astype(BF16)


def dot(a, b):
    return lax.dot_general(a, b, (((1,), (0,)), ((), ())), preferred_element_type=F32)


def dot_t(a, b):
    return lax.dot_general(a, b, (((1,), (1,)), ((), ())), preferred_element_type=F32)


def wide(x, times):
    return jnp.concatenate([x] * times, axis=1)


def kernel(
    n, nh, model, cg, rg, rh, w, ph,
    res, kgate, qgate, gain, filt, cot, query, keys, values, dout, docs,
    dnh, dnl, dfh, dfl, eh, el,
    g_res, g_kg, g_qg, g_gain, g_filt, g_q, g_k, g_v,
    inner_s, inner_h, gated_s, gated_h, f_s, g_s, gs_s,
    kvd, qt, dt, qf, df, dq, sbuf, rbuf, rs_src, y_dst, z_src, rs_dst, ag, sq, al,
    in_ss, in_rs, ga_ss, ga_rs, kv_ss, kv_rs, dk_ss, dk_rs, rs_ss, rs_rs, ag_ss, ag_rs, fb_ss, fb_rs,
    y_ss, y_rs, sq_ss, sq_rs, al_ss, al_rs,
):
    me = lax.axis_index("seq")
    hd = lax.axis_index("head")
    rows, channels = res.shape
    chunks = channels // CHUNK
    heads = query.shape[1] // HEAD
    scale = HEAD ** (-0.5)

    def cols(c):
        return pl.ds(pl.multiple_of(c * CHUNK, CHUNK), CHUNK)

    def remote(src, dst, ss, rs, seq, head):
        return pltpu.make_async_remote_copy(
            src_ref=src, dst_ref=dst, send_sem=ss, recv_sem=rs,
            device_id=(seq, head), device_id_type=MESH,
        )

    def each(count, body):
        def step(j, _):
            body(j)
            return 0
        lax.fori_loop(0, count, step, 0)

    def others(count, mine, body):
        def step(j):
            @pl.when(j != mine)
            def _():
                body(j)
        each(count, step)

    barrier = pltpu.get_barrier_semaphore()
    others(n, me, lambda j: pl.semaphore_signal(barrier, inc=1, device_id=(j, hd), device_id_type=MESH))
    others(nh, hd, lambda j: pl.semaphore_signal(barrier, inc=1, device_id=(me, j), device_id_type=MESH))

    kvd[me, 0:rows, :] = keys[...]
    kvd[me, rows : 2 * rows, :] = values[...]
    kvd[me, 2 * rows : 2 * rows + 16, :] = jnp.broadcast_to(docs[...].astype(F32), (16, rows)).astype(BF16)

    def square_step(i, acc):
        x = res[:, pl.ds(pl.multiple_of(i * 128, 128), 128)].astype(F32)
        return acc + x * x

    part = lax.fori_loop(0, channels // 128, square_step, jnp.zeros((rows, 128), F32))
    sq[hd] = jnp.broadcast_to(jnp.sum(part.T, axis=0, keepdims=True), (8, rows))

    pl.semaphore_wait(barrier, n - 1 + nh - 1)

    def sq_copy(slot, peer):
        return remote(sq.at[slot], sq.at[slot], sq_ss.at[peer], sq_rs.at[slot], me, peer)

    def al_copy(slot, peer):
        return remote(al.at[slot], al.at[slot], al_ss.at[peer], al_rs.at[slot], me, peer)

    def kv_copy(slot, peer):
        return remote(kvd.at[slot], kvd.at[slot], kv_ss.at[peer], kv_rs.at[slot], peer, hd)

    others(nh, hd, lambda j: sq_copy(hd, j).start())

    prev = jnp.maximum(me - 1, 0)
    succ = jnp.minimum(me + 1, n - 1)

    def in_copy(c):
        return remote(inner_s.at[c], inner_h.at[c], in_ss.at[c], in_rs.at[c], prev, hd)

    def ga_copy(c):
        return remote(gated_s.at[c], gated_h.at[c], ga_ss.at[c], ga_rs.at[c], succ, hd)

    def make_inner(c):
        inner_s[c] = (cot[:, cols(c)].astype(F32) * qgate[:, cols(c)].astype(F32)).astype(BF16)

        @pl.when(me > 0)
        def _():
            in_copy(c).start()
    each(chunks, make_inner)


    @pl.when(me == n - 1)
    def _():
        inner_h[...] = jnp.zeros_like(inner_h)

    @pl.when(me == 0)
    def _():
        gated_h[...] = jnp.zeros_like(gated_h)

    def send_kv(j):
        @pl.when(j > me)
        def _():
            kv_copy(me, j).start()
    each(n, send_kv)

    def filter_spectrum(c):
        block = filt[pl.ds(pl.multiple_of(c * CHUNK, CHUNK), CHUNK), :]
        fh, fl = split(block)
        f_s[c] = dot_t(dnh[...], fh) + (dot_t(dnh[...], fl) + dot_t(dnl[...], fh))
    each(chunks, filter_spectrum)

    others(nh, hd, lambda j: sq_copy(j, j).wait_recv())
    total = sq[0]
    for j in range(1, nh):
        total = total + sq[j]
    inv_row = lax.rsqrt(total * (1.0 / model) + NORM_EPS)
    inv = jnp.broadcast_to(inv_row[0:1, :], (128, rows)).T

    def norm_of(c):
        return res[:, cols(c)].astype(F32) * wide(inv, CHUNK // 128)

    def make_gated(c):
        scaled = norm_of(c) * gain[:, cols(c)]
        gated = (scaled * kgate[:, cols(c)].astype(F32)).astype(BF16)
        gated_s[c] = gated
        g_s[c] = dot(dnh[...], gated) + dot(dnl[...], gated)
    each(chunks, make_gated)

    par = lax.rem(me, 2)
    quarter = me // 2
    partner = me + 1 - 2 * par

    def half_copy(c):
        return remote(rs_src.at[1 - par, c], y_dst.at[c], y_ss.at[c], y_rs.at[c], partner, hd)

    def rs_copy(c, i, slot):
        m = c * ph + i
        return remote(z_src.at[c, i], rs_dst.at[slot], rs_ss.at[m], rs_rs.at[slot], 2 * m + par, hd)

    def ag_copy(slot, j):
        return remote(ag.at[slot], ag.at[slot], ag_ss.at[j], ag_rs.at[slot], 2 * j + par, hd)

    def fb_copy(slot):
        return remote(ag.at[slot], ag.at[slot], fb_ss.at[slot], fb_rs.at[slot], partner, hd)

    def merge(c):
        half_copy(c).wait_recv()
        z_src[c] = (rs_src[par, c].astype(F32) + y_dst[c].astype(F32)).astype(BF16)
        for i in range(ph):
            @pl.when(c * ph + i != quarter)
            def _():
                rs_copy(c, i, quarter).start()

    inv_h = jnp.concatenate([eh[0:rows, :], eh[rows : 2 * rows, :]], axis=1)
    inv_l = jnp.concatenate([el[0:rows, :], el[rows : 2 * rows, :]], axis=1)

    def synth(re, im):
        sh, sl = split(jnp.concatenate([re, im], axis=0))
        return dot(inv_h, sh) + (dot(inv_h, sl) + dot(inv_l, sh))

    def back_step(c, acc):
        @pl.when(me < n - 1)
        def _():
            in_copy(c).wait_recv()
        mine = inner_s[c]
        far = inner_h[c]
        u = (dot(dnh[...], mine) + dot(dfh[...], far)) + (dot(dnl[...], mine) + dot(dfl[...], far))
        ur, ui = u[:rows], u[rows:]
        gr, gi = g_s[c, 0:rows, :], g_s[c, rows : 2 * rows, :]
        taps = synth(ur * gr + ui * gi, ui * gr - ur * gi)
        fr, fi = f_s[c, 0:rows, :], f_s[c, rows : 2 * rows, :]
        back = synth(ur * fr + ui * fi, ui * fr - ur * fi)
        normed = norm_of(c)
        weight = gain[:, cols(c)]
        g_kg[:, cols(c)] = (back * (normed * weight)).astype(BF16)
        gs = back * kgate[:, cols(c)].astype(F32)
        gs_s[c] = gs
        prod = gs * normed
        gain_row = jnp.sum(prod, axis=0, keepdims=True)
        full = jnp.concatenate([taps, jnp.broadcast_to(gain_row, (rg * rh - rows, CHUNK))], axis=0).astype(BF16)
        per = CHUNK // w
        for a in range(per):
            for r in range(rg):
                at = a * rg + r
                rs_src[at % 2, c, at // 2] = full[r * rh : (r + 1) * rh, a * w : (a + 1) * w]
        half_copy(c).start()

        @pl.when(c > 0)
        def _():
            merge(c - 1)
        prod = prod * weight
        for a in range(CHUNK // 128):
            acc = acc + prod[:, a * 128 : (a + 1) * 128]
        return acc

    along = lax.fori_loop(0, chunks, back_step, jnp.zeros((rows, 128), F32))
    al[hd] = jnp.broadcast_to(jnp.sum(along.T, axis=0, keepdims=True), (8, rows))
    others(nh, hd, lambda j: al_copy(hd, j).start())

    merge(chunks - 1)

    def send_gated(c):
        @pl.when(me < n - 1)
        def _():
            ga_copy(c).start()
    each(chunks, send_gated)

    for h in range(heads):
        span = slice(h * HEAD, (h + 1) * HEAD)
        span_rows = slice(h * rows, (h + 1) * rows)
        q = query[:, span]
        d = dout[:, span]
        qf[span_rows, :] = q
        df[span_rows, :] = d
        qt[:, span_rows] = q.astype(F32).T.astype(BF16)
        dt[:, span_rows] = d.astype(F32).T.astype(BF16)

    my_docs = jnp.broadcast_to(docs[...].astype(F32), (rows, rows))
    row_at = lax.broadcasted_iota(jnp.int32, (rows, rows), 0)
    col_at = lax.broadcasted_iota(jnp.int32, (rows, rows), 1)

    def scores_of(j):
        key_docs = jnp.broadcast_to(kvd[j, 2 * rows : 2 * rows + 16, :].astype(F32)[0:1, :], (rows, rows)).T
        allowed = (key_docs == my_docs) & ((row_at <= col_at) | (j < me))
        bias = jnp.where(allowed, 0.0, FLOOR)
        return dot(kvd[j, 0:rows, :], qt[...]) * scale + wide(bias, heads)

    def wait_kv(j):
        @pl.when(j < me)
        def _():
            kv_copy(j, j).wait_recv()

    def max_step(j, top):
        wait_kv(j)
        return jnp.maximum(top, jnp.max(scores_of(j), axis=0, keepdims=True))

    flat = heads * rows
    top = lax.fori_loop(0, me + 1, max_step, jnp.full((1, flat), FLOOR, F32))

    def sum_step(j, state):
        total_p, total_w = state
        p = jnp.exp(scores_of(j) - top)
        dp = dot(kvd[j, rows : 2 * rows, :], dt[...])
        return (
            total_p + jnp.sum(p, axis=0, keepdims=True),
            total_w + jnp.sum(p * dp, axis=0, keepdims=True),
        )

    zero = jnp.zeros((1, flat), F32)
    total_p, total_w = lax.fori_loop(0, me + 1, sum_step, (zero, zero))
    inv_p = 1.0 / total_p
    delta = total_w * inv_p

    def rs_step(j, acc):
        rs_copy(j // ph, lax.rem(j, ph), j).wait_recv()
        return acc + rs_dst[j].astype(F32)

    mine = z_src[quarter // ph, lax.rem(quarter, ph)].astype(F32)
    mine = lax.fori_loop(0, quarter, rs_step, mine)
    mine = lax.fori_loop(quarter + 1, n // 2, rs_step, mine)
    ag[me] = mine.astype(BF16)
    others(n // 2, quarter, lambda j: ag_copy(me, j).start())
    fb_copy(me).start()

    dq[...] = jnp.zeros_like(dq)

    def dk_copy(peer, slot):
        return remote(sbuf.at[peer], rbuf.at[slot], dk_ss.at[peer], dk_rs.at[slot], peer, hd)

    def grad_step(j, acc):
        p = jnp.exp(scores_of(j) - top) * inv_p
        dp = dot(kvd[j, rows : 2 * rows, :], dt[...])
        ds = (p * (dp - delta)).astype(BF16)
        dv = dot(p.astype(BF16), df[...])
        dk = dot(ds, qf[...]) * scale
        key_t = kvd[j, 0:rows, :].astype(F32).T.astype(BF16)
        dq[...] += dot(key_t, ds)
        both = jnp.concatenate([dk, dv], axis=0)
        sbuf[j] = both.astype(BF16)

        @pl.when(j < me)
        def _():
            dk_copy(j, me).start()
        return both

    own = lax.fori_loop(0, me + 1, grad_step, jnp.zeros((2 * rows, HEAD), F32))
    for h in range(heads):
        g_q[:, h * HEAD : (h + 1) * HEAD] = (dq[:, h * rows : (h + 1) * rows].T * scale).astype(BF16)

    others(nh, hd, lambda j: al_copy(j, j).wait_recv())
    along_sum = al[0]
    for j in range(1, nh):
        along_sum = along_sum + al[j]
    along_col = jnp.broadcast_to(along_sum[0:1, :] * (1.0 / model), (128, rows)).T

    def res_step(c):
        times = CHUNK // 128
        out = gain[:, cols(c)] * gs_s[c] - norm_of(c) * wide(along_col, times)
        g_res[:, cols(c)] = (wide(inv, times) * out).astype(BF16)
    each(chunks, res_step)

    def query_gate_step(c):
        @pl.when(me > 0)
        def _():
            ga_copy(c).wait_recv()
        far = gated_h[c]
        wv = g_s[c] - (dot(dfh[...], far) + dot(dfl[...], far))
        wr, wi = wv[:rows], wv[rows:]
        fr, fi = f_s[c, 0:rows, :], f_s[c, rows : 2 * rows, :]
        filtered = synth(wr * fr - wi * fi, wr * fi + wi * fr)
        g_qg[:, cols(c)] = (cot[:, cols(c)].astype(F32) * filtered).astype(BF16)
    each(chunks, query_gate_step)

    def forward(j):
        slot = 2 * j + par
        ag_copy(slot, j).wait_recv()
        fb_copy(slot).start()
    others(n // 2, quarter, forward)

    def dk_step(j, acc):
        dk_copy(j, j).wait_recv()
        return acc + rbuf[j].astype(F32)

    own = lax.fori_loop(me + 1, n, dk_step, own)
    g_k[...] = own[:rows].astype(BF16)
    g_v[...] = own[rows:].astype(BF16)

    each(n // 2, lambda j: fb_copy(2 * j + 1 - par).wait_recv())

    def out_step(g):
        full = jnp.concatenate([ag[g * rg + r].astype(F32) for r in range(rg)], axis=0)
        g_filt[pl.ds(pl.multiple_of(g * w, w), w), :] = full[:rows].T
        g_gain[:, pl.ds(pl.multiple_of(g * w, w), w)] = full[rows : rows + 1]
    each(cg, out_step)

    others(nh, hd, lambda j: sq_copy(hd, j).wait_send())
    others(nh, hd, lambda j: al_copy(hd, j).wait_send())

    def sent_kv(j):
        @pl.when(j > me)
        def _():
            kv_copy(me, j).wait_send()

        @pl.when(j < me)
        def _():
            dk_copy(j, me).wait_send()
    each(n, sent_kv)

    def sent_halo(c):
        @pl.when(me > 0)
        def _():
            in_copy(c).wait_send()

        @pl.when(me < n - 1)
        def _():
            ga_copy(c).wait_send()
    each(chunks, sent_halo)
    each(chunks, lambda c: half_copy(c).wait_send())
    others(n // 2, quarter, lambda m: rs_copy(m // ph, lax.rem(m, ph), quarter).wait_send())
    others(n // 2, quarter, lambda j: ag_copy(me, j).wait_send())
    each(n // 2, lambda j: fb_copy(2 * j + par).wait_send())


def settle(count, *refs):
    held = refs[2 * count : 3 * count]
    into, out = refs[3 * count :]
    first = [pltpu.make_async_copy(refs[i], held[i], into.at[i]) for i in range(count)]
    second = [pltpu.make_async_copy(held[i], refs[count + i], out.at[i]) for i in range(count)]
    for copy in first:
        copy.start()
    for i in range(count):
        first[i].wait()
        second[i].start()
    for copy in second:
        copy.wait()


def on_device(n, nh, *args):
    (res, kgate, qgate, gain, filt, cot, query, keys, values, dout, docs) = args
    rows, channels = res.shape
    heads = query.shape[1] // HEAD
    chunks = channels // CHUNK
    cg = min(n, channels // 128)
    rg = n // cg
    w = channels // cg
    rh = -(-(filt.shape[1] + 1) // (16 * rg)) * 16
    ph = n // (2 * chunks)
    size = 2 * rows
    flat = heads * rows
    tables = [jnp.asarray(t) for t in dft_tables(rows)]
    vmem = pl.BlockSpec(memory_space=pltpu.VMEM)
    dma = pltpu.SemaphoreType.DMA
    outs = (
        jax.ShapeDtypeStruct(res.shape, BF16),
        jax.ShapeDtypeStruct(res.shape, BF16),
        jax.ShapeDtypeStruct(res.shape, BF16),
        jax.ShapeDtypeStruct((1, channels), F32),
        jax.ShapeDtypeStruct(filt.shape, F32),
        jax.ShapeDtypeStruct(query.shape, BF16),
        jax.ShapeDtypeStruct(keys.shape, BF16),
        jax.ShapeDtypeStruct(values.shape, BF16),
    )
    block = (chunks, rows, CHUNK)
    scratch = [
        pltpu.VMEM(block, BF16),
        pltpu.VMEM(block, BF16),
        pltpu.VMEM(block, BF16),
        pltpu.VMEM(block, BF16),
        pltpu.VMEM((chunks, size, CHUNK), F32),
        pltpu.VMEM((chunks, size, CHUNK), F32),
        pltpu.VMEM(block, F32),
        pltpu.VMEM((n, size + 16, HEAD), BF16),
        pltpu.VMEM((HEAD, flat), BF16),
        pltpu.VMEM((HEAD, flat), BF16),
        pltpu.VMEM((flat, HEAD), BF16),
        pltpu.VMEM((flat, HEAD), BF16),
        pltpu.VMEM((HEAD, flat), F32),
        pltpu.VMEM((n, size, HEAD), BF16),
        pltpu.VMEM((n, size, HEAD), BF16),
        pltpu.VMEM((2, chunks, ph, rh, w), BF16),
        pltpu.VMEM((chunks, ph, rh, w), BF16),
        pltpu.VMEM((chunks, ph, rh, w), BF16),
        pltpu.VMEM((n // 2, rh, w), BF16),
        pltpu.VMEM((n, rh, w), BF16),
        pltpu.VMEM((nh, 8, rows), F32),
        pltpu.VMEM((nh, 8, rows), F32),
    ]
    scratch += [dma((chunks,))] * 4 + [dma((n,))] * 10 + [dma((chunks,))] * 2 + [dma((nh,))] * 4
    result = pl.pallas_call(
        functools.partial(kernel, n, nh, nh * channels, cg, rg, rh, w, ph),
        out_shape=outs,
        in_specs=[vmem] * (11 + len(tables)),
        out_specs=(vmem,) * len(outs),
        scratch_shapes=scratch,
        compiler_params=pltpu.CompilerParams(
            collective_id=0, has_side_effects=True, vmem_limit_bytes=56 * 1024 * 1024
        ),
        name="hyena_attention_backward",
    )(
        res, kgate, qgate, gain.reshape(1, channels), filt, cot, query, keys, values, dout,
        docs.reshape(1, rows), *tables,
    )
    anywhere = pl.BlockSpec(memory_space=pl.ANY)
    result = pl.pallas_call(
        functools.partial(settle, len(outs)),
        out_shape=outs,
        in_specs=[anywhere] * len(outs),
        out_specs=(anywhere,) * len(outs),
        scratch_shapes=[pltpu.VMEM(o.shape, o.dtype) for o in outs] + [dma((len(outs),))] * 2,
        compiler_params=pltpu.CompilerParams(vmem_limit_bytes=56 * 1024 * 1024),
        name="settle_outputs",
    )(*result)
    return result[:3] + (result[3].reshape(channels),) + result[4:]


def solution(mesh):
    n, nh = mesh.shape["seq"], mesh.shape["head"]
    rows = P("seq", "head")
    return jax.shard_map(
        functools.partial(on_device, n, nh),
        mesh=mesh,
        in_specs=(rows, rows, rows, P("head"), P("head", None), rows, rows, rows, rows, rows, P("seq")),
        out_specs=(rows, rows, rows, P("head"), P("head", None), rows, rows, rows),
        check_vma=False,
    )
```

```python
import functools

import jax
import jax.numpy as jnp
import ml_dtypes
import numpy as np
from jax import lax
from jax.experimental import pallas as pl
from jax.experimental.pallas import tpu as pltpu
from jax.sharding import PartitionSpec as P

HEAD = 128
NORM_EPS = 1e-05
FLOOR = -1e30
CHUNK = 512
F32 = jnp.float32
BF16 = jnp.bfloat16
MESH = pl.DeviceIdType.MESH


def split_const(x):
    high = x.astype(ml_dtypes.bfloat16)
    low = (x - high.astype(np.float64)).astype(ml_dtypes.bfloat16)
    return high, low


def dft_tables(rows):
    size = 2 * rows
    freq = 2 * np.pi * (np.arange(rows) + 0.5) / size
    angle = freq[:, None] * np.arange(size)[None, :]
    forward = np.concatenate([np.cos(angle), -np.sin(angle)], 0)
    wave = angle[:, :rows].T
    back = np.concatenate([np.cos(wave), -np.sin(wave)], 0) * (2.0 / size)
    near = split_const(forward[:, :rows])
    far = split_const(forward[:, rows:])
    inverse = split_const(back)
    return near + far + inverse


def split(x):
    high = x.astype(BF16)
    return high, (x - high.astype(F32)).astype(BF16)


def dot(a, b):
    return lax.dot_general(a, b, (((1,), (0,)), ((), ())), preferred_element_type=F32)


def dot_t(a, b):
    return lax.dot_general(a, b, (((1,), (1,)), ((), ())), preferred_element_type=F32)


def wide(x, times):
    return jnp.concatenate([x] * times, axis=1)


def kernel(
    n, nh, model, cg, rg, rh, w, ph,
    res, kgate, qgate, gain, filt, cot, query, keys, values, dout, docs,
    dnh, dnl, dfh, dfl, eh, el,
    o_res, o_kg, o_qg, g_gain, g_filt, o_q, g_k, g_v,
    g_res, g_kg, g_qg, g_q, out_sem,
    inner_s, inner_h, gated_s, gated_h, f_s, g_s, u_s, gs_s,
    kvd, qt, dt, qf, df, dq, sbuf, rbuf, rs_src, y_dst, z_src, rs_dst, ag, sq, al,
    in_ss, in_rs, ga_ss, ga_rs, kv_ss, kv_rs, dk_ss, dk_rs, rs_ss, rs_rs, ag_ss, ag_rs, fb_ss, fb_rs,
    y_ss, y_rs, sq_ss, sq_rs, al_ss, al_rs,
):
    me = lax.axis_index("seq")
    hd = lax.axis_index("head")
    rows, channels = res.shape
    chunks = channels // CHUNK
    heads = query.shape[1] // HEAD
    scale = HEAD ** (-0.5)

    def cols(c):
        return pl.ds(pl.multiple_of(c * CHUNK, CHUNK), CHUNK)

    def remote(src, dst, ss, rs, seq, head):
        return pltpu.make_async_remote_copy(
            src_ref=src, dst_ref=dst, send_sem=ss, recv_sem=rs,
            device_id=(seq, head), device_id_type=MESH,
        )

    def each(count, body):
        def step(j, _):
            body(j)
            return 0
        lax.fori_loop(0, count, step, 0)

    def others(count, mine, body):
        def step(j):
            @pl.when(j != mine)
            def _():
                body(j)
        each(count, step)

    def leave(i):
        held = (g_res, g_kg, g_qg, g_q)[i]
        out = (o_res, o_kg, o_qg, o_q)[i]
        return pltpu.make_async_copy(held, out, out_sem.at[i])

    barrier = pltpu.get_barrier_semaphore()
    others(n, me, lambda j: pl.semaphore_signal(barrier, inc=1, device_id=(j, hd), device_id_type=MESH))
    others(nh, hd, lambda j: pl.semaphore_signal(barrier, inc=1, device_id=(me, j), device_id_type=MESH))

    prev = jnp.maximum(me - 1, 0)
    succ = jnp.minimum(me + 1, n - 1)

    def in_copy(c):
        return remote(inner_s.at[c], inner_h.at[c], in_ss.at[c], in_rs.at[c], prev, hd)

    def ga_copy(c):
        return remote(gated_s.at[c], gated_h.at[c], ga_ss.at[c], ga_rs.at[c], succ, hd)

    def make_inner(c):
        inner_s[c] = (cot[:, cols(c)].astype(F32) * qgate[:, cols(c)].astype(F32)).astype(BF16)
    each(chunks, make_inner)

    pl.semaphore_wait(barrier, n - 1 + nh - 1)

    def send_inner(c):
        @pl.when(me > 0)
        def _():
            in_copy(c).start()
    each(chunks, send_inner)

    kvd[me, 0:rows, :] = keys[...]
    kvd[me, rows : 2 * rows, :] = values[...]
    kvd[me, 2 * rows : 2 * rows + 16, :] = jnp.broadcast_to(docs[...].astype(F32), (16, rows)).astype(BF16)

    def square_step(i, acc):
        x = res[:, pl.ds(pl.multiple_of(i * 128, 128), 128)].astype(F32)
        return acc + x * x

    part = lax.fori_loop(0, channels // 128, square_step, jnp.zeros((rows, 128), F32))
    sq[hd] = jnp.broadcast_to(jnp.sum(part.T, axis=0, keepdims=True), (8, rows))

    def sq_copy(slot, peer):
        return remote(sq.at[slot], sq.at[slot], sq_ss.at[peer], sq_rs.at[slot], me, peer)

    def al_copy(slot, peer):
        return remote(al.at[slot], al.at[slot], al_ss.at[peer], al_rs.at[slot], me, peer)

    def kv_copy(slot, peer):
        return remote(kvd.at[slot], kvd.at[slot], kv_ss.at[peer], kv_rs.at[slot], peer, hd)

    others(nh, hd, lambda j: sq_copy(hd, j).start())

    @pl.when(me == n - 1)
    def _():
        inner_h[...] = jnp.zeros_like(inner_h)

    @pl.when(me == 0)
    def _():
        gated_h[...] = jnp.zeros_like(gated_h)

    def send_kv(j):
        @pl.when(j > me)
        def _():
            kv_copy(me, j).start()
    each(n, send_kv)

    def filter_spectrum(c):
        block = filt[pl.ds(pl.multiple_of(c * CHUNK, CHUNK), CHUNK), :]
        fh, fl = split(block)
        u_s[c] = dot(dnh[...], inner_s[c]) + dot(dnl[...], inner_s[c])
        f_s[c] = dot_t(dnh[...], fh) + (dot_t(dnh[...], fl) + dot_t(dnl[...], fh))
    each(chunks, filter_spectrum)

    others(nh, hd, lambda j: sq_copy(j, j).wait_recv())
    total = sq[0]
    for j in range(1, nh):
        total = total + sq[j]
    inv_row = lax.rsqrt(total * (1.0 / model) + NORM_EPS)
    inv = jnp.broadcast_to(inv_row[0:1, :], (128, rows)).T

    def norm_of(c):
        return res[:, cols(c)].astype(F32) * wide(inv, CHUNK // 128)

    def make_gated(c):
        scaled = norm_of(c) * gain[:, cols(c)]
        gated = (scaled * kgate[:, cols(c)].astype(F32)).astype(BF16)
        gated_s[c] = gated
        g_s[c] = dot(dnh[...], gated) + dot(dnl[...], gated)
    each(chunks, make_gated)

    par = lax.rem(me, 2)
    quarter = me // 2
    partner = me + 1 - 2 * par

    def half_copy(c):
        return remote(rs_src.at[1 - par, c], y_dst.at[c], y_ss.at[c], y_rs.at[c], partner, hd)

    def rs_copy(c, i, slot):
        m = c * ph + i
        return remote(z_src.at[c, i], rs_dst.at[slot], rs_ss.at[m], rs_rs.at[slot], 2 * m + par, hd)

    def ag_copy(slot, j):
        return remote(ag.at[slot], ag.at[slot], ag_ss.at[j], ag_rs.at[slot], 2 * j + par, hd)

    def fb_copy(slot):
        return remote(ag.at[slot], ag.at[slot], fb_ss.at[slot], fb_rs.at[slot], partner, hd)

    def merge(c):
        half_copy(c).wait_recv()
        z_src[c] = (rs_src[par, c].astype(F32) + y_dst[c].astype(F32)).astype(BF16)
        for i in range(ph):
            @pl.when(c * ph + i != quarter)
            def _():
                rs_copy(c, i, quarter).start()

    inv_h = jnp.concatenate([eh[0:rows, :], eh[rows : 2 * rows, :]], axis=1)
    inv_l = jnp.concatenate([el[0:rows, :], el[rows : 2 * rows, :]], axis=1)

    def synth(re, im):
        sh, sl = split(jnp.concatenate([re, im], axis=0))
        return dot(inv_h, sh) + (dot(inv_h, sl) + dot(inv_l, sh))

    def back_step(c, acc):
        @pl.when(me < n - 1)
        def _():
            in_copy(c).wait_recv()
        far = inner_h[c]
        u = u_s[c] + (dot(dfh[...], far) + dot(dfl[...], far))
        ur, ui = u[:rows], u[rows:]
        gr, gi = g_s[c, 0:rows, :], g_s[c, rows : 2 * rows, :]
        taps = synth(ur * gr + ui * gi, ui * gr - ur * gi)
        fr, fi = f_s[c, 0:rows, :], f_s[c, rows : 2 * rows, :]
        back = synth(ur * fr + ui * fi, ui * fr - ur * fi)
        normed = norm_of(c)
        weight = gain[:, cols(c)]
        g_kg[:, cols(c)] = (back * (normed * weight)).astype(BF16)
        gs = back * kgate[:, cols(c)].astype(F32)
        gs_s[c] = gs
        prod = gs * normed
        gain_row = jnp.sum(prod, axis=0, keepdims=True)
        full = jnp.concatenate([taps, jnp.broadcast_to(gain_row, (rg * rh - rows, CHUNK))], axis=0).astype(BF16)
        per = CHUNK // w
        for a in range(per):
            for r in range(rg):
                at = a * rg + r
                rs_src[at % 2, c, at // 2] = full[r * rh : (r + 1) * rh, a * w : (a + 1) * w]
        half_copy(c).start()

        @pl.when(c > 0)
        def _():
            merge(c - 1)
        prod = prod * weight
        for a in range(CHUNK // 128):
            acc = acc + prod[:, a * 128 : (a + 1) * 128]
        return acc

    along = lax.fori_loop(0, chunks, back_step, jnp.zeros((rows, 128), F32))
    al[hd] = jnp.broadcast_to(jnp.sum(along.T, axis=0, keepdims=True), (8, rows))
    others(nh, hd, lambda j: al_copy(hd, j).start())

    merge(chunks - 1)
    leave(1).start()

    def send_gated(c):
        @pl.when(me < n - 1)
        def _():
            ga_copy(c).start()
    each(chunks, send_gated)

    for h in range(heads):
        span = slice(h * HEAD, (h + 1) * HEAD)
        span_rows = slice(h * rows, (h + 1) * rows)
        q = query[:, span]
        d = dout[:, span]
        qf[span_rows, :] = q
        df[span_rows, :] = d
        qt[:, span_rows] = q.astype(F32).T.astype(BF16)
        dt[:, span_rows] = d.astype(F32).T.astype(BF16)

    my_docs = jnp.broadcast_to(docs[...].astype(F32), (rows, rows))
    row_at = lax.broadcasted_iota(jnp.int32, (rows, rows), 0)
    col_at = lax.broadcasted_iota(jnp.int32, (rows, rows), 1)

    def scores_of(j):
        key_docs = jnp.broadcast_to(kvd[j, 2 * rows : 2 * rows + 16, :].astype(F32)[0:1, :], (rows, rows)).T
        allowed = (key_docs == my_docs) & ((row_at <= col_at) | (j < me))
        bias = jnp.where(allowed, 0.0, FLOOR)
        return dot(kvd[j, 0:rows, :], qt[...]) * scale + wide(bias, heads)

    def wait_kv(j):
        @pl.when(j < me)
        def _():
            kv_copy(j, j).wait_recv()

    def max_step(j, top):
        wait_kv(j)
        return jnp.maximum(top, jnp.max(scores_of(j), axis=0, keepdims=True))

    flat = heads * rows
    top = lax.fori_loop(0, me + 1, max_step, jnp.full((1, flat), FLOOR, F32))

    def sum_step(j, state):
        total_p, total_w = state
        p = jnp.exp(scores_of(j) - top)
        dp = dot(kvd[j, rows : 2 * rows, :], dt[...])
        return (
            total_p + jnp.sum(p, axis=0, keepdims=True),
            total_w + jnp.sum(p * dp, axis=0, keepdims=True),
        )

    zero = jnp.zeros((1, flat), F32)
    total_p, total_w = lax.fori_loop(0, me + 1, sum_step, (zero, zero))
    inv_p = 1.0 / total_p
    delta = total_w * inv_p

    def rs_step(j, acc):
        rs_copy(j // ph, lax.rem(j, ph), j).wait_recv()
        return acc + rs_dst[j].astype(F32)

    mine = z_src[quarter // ph, lax.rem(quarter, ph)].astype(F32)
    mine = lax.fori_loop(0, quarter, rs_step, mine)
    mine = lax.fori_loop(quarter + 1, n // 2, rs_step, mine)
    ag[me] = mine.astype(BF16)
    others(n // 2, quarter, lambda j: ag_copy(me, j).start())
    fb_copy(me).start()

    dq[...] = jnp.zeros_like(dq)

    def dk_copy(peer, slot):
        return remote(sbuf.at[peer], rbuf.at[slot], dk_ss.at[peer], dk_rs.at[slot], peer, hd)

    def grad_step(j, acc):
        p = jnp.exp(scores_of(j) - top) * inv_p
        dp = dot(kvd[j, rows : 2 * rows, :], dt[...])
        ds = (p * (dp - delta)).astype(BF16)
        dv = dot(p.astype(BF16), df[...])
        dk = dot(ds, qf[...]) * scale
        key_t = kvd[j, 0:rows, :].astype(F32).T.astype(BF16)
        dq[...] += dot(key_t, ds)
        both = jnp.concatenate([dk, dv], axis=0)
        sbuf[j] = both.astype(BF16)

        @pl.when(j < me)
        def _():
            dk_copy(j, me).start()
        return both

    own = lax.fori_loop(0, me + 1, grad_step, jnp.zeros((2 * rows, HEAD), F32))
    for h in range(heads):
        g_q[:, h * HEAD : (h + 1) * HEAD] = (dq[:, h * rows : (h + 1) * rows].T * scale).astype(BF16)

    def forward(j):
        slot = 2 * j + par
        ag_copy(slot, j).wait_recv()
        fb_copy(slot).start()
    others(n // 2, quarter, forward)

    leave(3).start()

    others(nh, hd, lambda j: al_copy(j, j).wait_recv())
    along_sum = al[0]
    for j in range(1, nh):
        along_sum = along_sum + al[j]
    along_col = jnp.broadcast_to(along_sum[0:1, :] * (1.0 / model), (128, rows)).T

    def res_step(c):
        times = CHUNK // 128
        out = gain[:, cols(c)] * gs_s[c] - norm_of(c) * wide(along_col, times)
        g_res[:, cols(c)] = (wide(inv, times) * out).astype(BF16)
    each(chunks, res_step)
    leave(0).start()

    def query_gate_step(c):
        @pl.when(me > 0)
        def _():
            ga_copy(c).wait_recv()
        far = gated_h[c]
        wv = g_s[c] - (dot(dfh[...], far) + dot(dfl[...], far))
        wr, wi = wv[:rows], wv[rows:]
        fr, fi = f_s[c, 0:rows, :], f_s[c, rows : 2 * rows, :]
        filtered = synth(wr * fr - wi * fi, wr * fi + wi * fr)
        g_qg[:, cols(c)] = (cot[:, cols(c)].astype(F32) * filtered).astype(BF16)
    each(chunks, query_gate_step)
    leave(2).start()

    def dk_step(j, acc):
        dk_copy(j, j).wait_recv()
        return acc + rbuf[j].astype(F32)

    own = lax.fori_loop(me + 1, n, dk_step, own)
    g_k[...] = own[:rows].astype(BF16)
    g_v[...] = own[rows:].astype(BF16)

    each(n // 2, lambda j: fb_copy(2 * j + 1 - par).wait_recv())

    def out_step(g):
        full = jnp.concatenate([ag[g * rg + r].astype(F32) for r in range(rg)], axis=0)
        g_filt[pl.ds(pl.multiple_of(g * w, w), w), :] = full[:rows].T
        g_gain[:, pl.ds(pl.multiple_of(g * w, w), w)] = full[rows : rows + 1]
    each(cg, out_step)

    for i in range(4):
        leave(i).wait()
    others(nh, hd, lambda j: sq_copy(hd, j).wait_send())
    others(nh, hd, lambda j: al_copy(hd, j).wait_send())

    def sent_kv(j):
        @pl.when(j > me)
        def _():
            kv_copy(me, j).wait_send()

        @pl.when(j < me)
        def _():
            dk_copy(j, me).wait_send()
    each(n, sent_kv)

    def sent_halo(c):
        @pl.when(me > 0)
        def _():
            in_copy(c).wait_send()

        @pl.when(me < n - 1)
        def _():
            ga_copy(c).wait_send()
    each(chunks, sent_halo)
    each(chunks, lambda c: half_copy(c).wait_send())
    others(n // 2, quarter, lambda m: rs_copy(m // ph, lax.rem(m, ph), quarter).wait_send())
    others(n // 2, quarter, lambda j: ag_copy(me, j).wait_send())
    each(n // 2, lambda j: fb_copy(2 * j + par).wait_send())


def settle(count, *refs):
    held = refs[2 * count : 3 * count]
    into, out = refs[3 * count :]
    first = [pltpu.make_async_copy(refs[i], held[i], into.at[i]) for i in range(count)]
    second = [pltpu.make_async_copy(held[i], refs[count + i], out.at[i]) for i in range(count)]
    for copy in first:
        copy.start()
    for i in range(count):
        first[i].wait()
        second[i].start()
    for copy in second:
        copy.wait()


def on_device(n, nh, *args):
    (res, kgate, qgate, gain, filt, cot, query, keys, values, dout, docs) = args
    rows, channels = res.shape
    heads = query.shape[1] // HEAD
    chunks = channels // CHUNK
    cg = min(n, channels // 128)
    rg = n // cg
    w = channels // cg
    rh = -(-(filt.shape[1] + 1) // (16 * rg)) * 16
    ph = n // (2 * chunks)
    size = 2 * rows
    flat = heads * rows
    tables = [jnp.asarray(t) for t in dft_tables(rows)]
    vmem = pl.BlockSpec(memory_space=pltpu.VMEM)
    anywhere = pl.BlockSpec(memory_space=pl.ANY)
    dma = pltpu.SemaphoreType.DMA
    outs = (
        jax.ShapeDtypeStruct(res.shape, BF16),
        jax.ShapeDtypeStruct(res.shape, BF16),
        jax.ShapeDtypeStruct(res.shape, BF16),
        jax.ShapeDtypeStruct((1, channels), F32),
        jax.ShapeDtypeStruct(filt.shape, F32),
        jax.ShapeDtypeStruct(query.shape, BF16),
        jax.ShapeDtypeStruct(keys.shape, BF16),
        jax.ShapeDtypeStruct(values.shape, BF16),
    )
    block = (chunks, rows, CHUNK)
    scratch = [
        pltpu.VMEM(res.shape, BF16),
        pltpu.VMEM(res.shape, BF16),
        pltpu.VMEM(res.shape, BF16),
        pltpu.VMEM(query.shape, BF16),
        dma((4,)),
        pltpu.VMEM(block, BF16),
        pltpu.VMEM(block, BF16),
        pltpu.VMEM(block, BF16),
        pltpu.VMEM(block, BF16),
        pltpu.VMEM((chunks, size, CHUNK), F32),
        pltpu.VMEM((chunks, size, CHUNK), F32),
        pltpu.VMEM((chunks, size, CHUNK), F32),
        pltpu.VMEM(block, F32),
        pltpu.VMEM((n, size + 16, HEAD), BF16),
        pltpu.VMEM((HEAD, flat), BF16),
        pltpu.VMEM((HEAD, flat), BF16),
        pltpu.VMEM((flat, HEAD), BF16),
        pltpu.VMEM((flat, HEAD), BF16),
        pltpu.VMEM((HEAD, flat), F32),
        pltpu.VMEM((n, size, HEAD), BF16),
        pltpu.VMEM((n, size, HEAD), BF16),
        pltpu.VMEM((2, chunks, ph, rh, w), BF16),
        pltpu.VMEM((chunks, ph, rh, w), BF16),
        pltpu.VMEM((chunks, ph, rh, w), BF16),
        pltpu.VMEM((n // 2, rh, w), BF16),
        pltpu.VMEM((n, rh, w), BF16),
        pltpu.VMEM((nh, 8, rows), F32),
        pltpu.VMEM((nh, 8, rows), F32),
    ]
    scratch += [dma((chunks,))] * 4 + [dma((n,))] * 10 + [dma((chunks,))] * 2 + [dma((nh,))] * 4
    result = pl.pallas_call(
        functools.partial(kernel, n, nh, nh * channels, cg, rg, rh, w, ph),
        out_shape=outs,
        in_specs=[vmem] * (11 + len(tables)),
        out_specs=(anywhere,) * 3 + (vmem,) * 2 + (anywhere,) + (vmem,) * 2,
        scratch_shapes=scratch,
        compiler_params=pltpu.CompilerParams(
            collective_id=0, has_side_effects=True, vmem_limit_bytes=56 * 1024 * 1024
        ),
        name="hyena_attention_backward",
    )(
        res, kgate, qgate, gain.reshape(1, channels), filt, cot, query, keys, values, dout,
        docs.reshape(1, rows), *tables,
    )
    result = pl.pallas_call(
        functools.partial(settle, len(outs)),
        out_shape=outs,
        in_specs=[anywhere] * len(outs),
        out_specs=(anywhere,) * len(outs),
        scratch_shapes=[pltpu.VMEM(o.shape, o.dtype) for o in outs] + [dma((len(outs),))] * 2,
        compiler_params=pltpu.CompilerParams(vmem_limit_bytes=56 * 1024 * 1024),
        name="settle_outputs",
    )(*result)
    return result[:3] + (result[3].reshape(channels),) + result[4:]


def solution(mesh):
    n, nh = mesh.shape["seq"], mesh.shape["head"]
    rows = P("seq", "head")
    return jax.shard_map(
        functools.partial(on_device, n, nh),
        mesh=mesh,
        in_specs=(rows, rows, rows, P("head"), P("head", None), rows, rows, rows, rows, rows, P("seq")),
        out_specs=(rows, rows, rows, P("head"), P("head", None), rows, rows, rows),
        check_vma=False,
    )
```
